32 devices in a mesh: energy: 8 (over z, x), mom: 4 (over y, core).
Axes of the slice: x: 2, y: 2, z: 4, core: 2. Of those that a mesh axis runs over, the one named last changes fastest.
Arguments:
- hamiltonian: float32 [4, 2, 3, 192, 192], P('mom'), may hold values from -0.109375 to 0.109375
- coupling: float32 [4, 2, 2, 192, 192], P('mom'), may hold values from -0.09375 to 0.09375
- sigma_old: float32 [16, 4, 2, 3, 192, 192], P('energy', 'mom'), may hold values from -1.5 to 0.5
- orbital_coupling: float32 [3, 192, 192], replicated, may hold values from 0.3 to 3
- momentum_weights: float32 [4, 4], replicated, may hold values from 0 to 2
- bose_factor: float32 [3], replicated, may hold values from 0.1 to 3
- shifts: int32 [3], replicated, may hold values from 1 to 2, as said below
Outputs:
- sigma_new: float32 [16, 4, 2, 3, 192, 192], P('energy', 'mom')
The draws below stay inside these ranges and needn't reach their ends.
Inputs may be any that keep to these rules, and one draw needn't show every extreme that they name: `shifts`: each mode's phonon energy in whole energy steps; some mode's shift equals 2.
All inputs are finite; a program needn't handle non-finite values.
Results may differ from the reference program's by a relative error of at most 0.0003.
Values sent between devices are 32-bit elements; how exact they have to be, the bound alone decides.
No kernel may reach another device: no remote copies, remote signals or barrier semaphores. Data moves between devices by JAX's collectives and lax.ppermute only.
A program may use at most 192 MiB of HBM per device.

```python
import math
import jax
import jax.numpy as jnp
from jax import lax

B = 192
SLABS = 3
MODES = 3
NS_STEPS = 3
E_ALL = 16
K_ALL = 4
SHIFT_MAX = 2


def draw_shifts(key, part):
    first_key, second_key = jax.random.split(jax.random.fold_in(key, 11))
    values = jax.random.randint(first_key, (MODES,), 1, SHIFT_MAX + 1)
    chosen = jax.random.randint(second_key, (), 0, MODES)
    return jnp.where(jnp.arange(MODES) == chosen, SHIFT_MAX, values).astype(jnp.int32)


def draw_sigma_old(key, part):
    noise_key, width_key, level_key = jax.random.split(jax.random.fold_in(key, 23), 3)
    full_shape = (E_ALL, K_ALL, 2, SLABS, B, B)
    diag_shape = (E_ALL, K_ALL, SLABS, B)
    noise = jax.random.normal(noise_key, full_shape, jnp.float32) * (0.2 / B ** 0.5)
    widths = jnp.exp(jax.random.uniform(width_key, diag_shape, jnp.float32, jnp.log(0.9), jnp.log(1.5)))
    widths = jnp.clip(widths, 0.9, 1.5)
    levels = jax.random.uniform(level_key, diag_shape, jnp.float32, -0.5, 0.5)
    identity = jnp.eye(B, dtype=jnp.float32)
    real_part = noise[:, :, 0] * (1.0 - identity) + levels[..., None] * identity
    imag_part = noise[:, :, 1] * (1.0 - identity) - widths[..., None] * identity
    return jnp.stack([real_part, imag_part], axis=2).astype(jnp.float32)


def block_scale(own_key, shape, pieces, smallest, top_value):
    level = 1.0
    for axis_at, parts in pieces:
        heights = jax.random.uniform(jax.random.fold_in(jax.random.fold_in(own_key, 6), axis_at), (parts,), jnp.float32, smallest / len(pieces), top_value / len(pieces))
        level = level * jnp.repeat(jnp.exp(heights), shape[axis_at] // parts).reshape((-1,) + (1,) * (len(shape) - 1 - axis_at))
    return level


def bell_draw(key, dims, scale, bound, shards=(), held_as=jnp.bfloat16):
    loudness = block_scale(key, dims, shards, -0.22, 0.18) if shards else 1.0
    drawn = jax.random.normal(key, dims, jnp.float32) * scale * loudness
    return jnp.minimum(jnp.maximum(drawn, -bound), bound).astype(held_as)


def setup_inputs(seed: int = 0) -> dict:
    key_of = jax.random.split(jax.random.key(seed), 8)
    hamiltonian = bell_draw(key_of[0], (K_ALL, 2, SLABS, B, B), (16 * B) ** -0.5, 0.109375, ((0, 4),), jnp.float32)
    coupling = bell_draw(key_of[1], (K_ALL, 2, SLABS - 1, B, B), (20 * B) ** -0.5, 0.09375, ((0, 4),), jnp.float32)
    sigma_old = draw_sigma_old(jax.random.fold_in(key_of[7], 71), 0)
    orbital_coupling = jnp.clip(jnp.exp(jax.random.uniform(key_of[3], (MODES, B, B), jnp.float32, math.log(0.3), math.log(3.0))), 0.3, 3.0)
    momentum_weights = jnp.clip(jax.random.uniform(key_of[4], (K_ALL, K_ALL), jnp.float32, 0.0, 2.0), 0.0, 2.0)
    bose_factor = jnp.clip(jnp.exp(jax.random.uniform(key_of[5], (MODES,), jnp.float32, math.log(0.1), math.log(3.0))), 0.1, 3.0)
    shifts = draw_shifts(jax.random.fold_in(key_of[7], 71), 0)
    return dict(hamiltonian=hamiltonian, coupling=coupling, sigma_old=sigma_old, orbital_coupling=orbital_coupling, momentum_weights=momentum_weights, bose_factor=bose_factor, shifts=shifts)


BROADENING = 0.05


def real_product(first_matrix, second_matrix):
    return jnp.dot(first_matrix, second_matrix, precision=lax.Precision.HIGHEST, preferred_element_type=jnp.float32)


def complex_product(first_pair, second_pair):
    real_part = real_product(first_pair[0], second_pair[0]) - real_product(first_pair[1], second_pair[1])
    imag_part = real_product(first_pair[0], second_pair[1]) + real_product(first_pair[1], second_pair[0])
    return (real_part, imag_part)


def adjoint(block_pair):
    return (block_pair[0].T, -block_pair[1].T)


def newton_inverse(matrix_pair):
    matrix_real, matrix_imag = matrix_pair
    identity = jnp.eye(matrix_real.shape[0], dtype=jnp.float32)
    diag_real = jnp.diagonal(matrix_real)
    diag_imag = jnp.diagonal(matrix_imag)
    modulus = diag_real * diag_real + diag_imag * diag_imag
    recip_real = diag_real / modulus
    recip_imag = -diag_imag / modulus
    scaled_real = matrix_real * recip_real[None, :] - matrix_imag * recip_imag[None, :]
    scaled_imag = matrix_real * recip_imag[None, :] + matrix_imag * recip_real[None, :]
    resid_real = 2.0 * identity - scaled_real
    resid_imag = -scaled_imag
    approx = (recip_real[:, None] * resid_real - recip_imag[:, None] * resid_imag,
              recip_real[:, None] * resid_imag + recip_imag[:, None] * resid_real)
    for newton_step in range(NS_STEPS - 1):
        product = complex_product(matrix_pair, approx)
        approx = complex_product(approx, (2.0 * identity - product[0], -product[1]))
    return approx


def hermitian_part(ham_real, ham_imag):
    return (0.5 * (ham_real + jnp.swapaxes(ham_real, 1, 2)), 0.5 * (ham_imag - jnp.swapaxes(ham_imag, 1, 2)))


def green_blocks(herm_real, herm_imag, link_real, link_imag, sigma_real, sigma_imag, energy):
    identity = jnp.eye(herm_real.shape[-1], dtype=jnp.float32)
    forward = []
    adjoint_side = []
    for slab_index in range(SLABS):
        system_real = energy * identity - herm_real[slab_index] - sigma_real[slab_index]
        system_imag = BROADENING * identity - herm_imag[slab_index] - sigma_imag[slab_index]
        if slab_index > 0:
            link_pair = (link_real[slab_index - 1], link_imag[slab_index - 1])
            leaving = complex_product(adjoint(link_pair), forward[-1])
            folded = complex_product(leaving, link_pair)
            adjoint_side.append(leaving)
            system_real = system_real - folded[0]
            system_imag = system_imag - folded[1]
        forward.append(newton_inverse((system_real, system_imag)))
    blocks = [forward[-1]]
    for slab_index in range(SLABS - 2, -1, -1):
        link_pair = (link_real[slab_index], link_imag[slab_index])
        outward = complex_product(forward[slab_index], link_pair)
        through = complex_product(outward, blocks[0])
        closing = complex_product(through, adjoint_side[slab_index])
        blocks.insert(0, (forward[slab_index][0] + closing[0], forward[slab_index][1] + closing[1]))
    return jnp.stack([jnp.stack([block_pair[0] for block_pair in blocks]), jnp.stack([block_pair[1] for block_pair in blocks])])


def phonon_sum(padded, energy_count, couplings, bose_factor, shifts, target_shape):
    running = jnp.zeros(target_shape, jnp.float32)
    for mode_index in range(couplings.shape[0]):
        below_shift = lax.dynamic_slice_in_dim(padded, SHIFT_MAX - shifts[mode_index], energy_count, 0).reshape(target_shape)
        above_shift = lax.dynamic_slice_in_dim(padded, SHIFT_MAX + shifts[mode_index], energy_count, 0).reshape(target_shape)
        running = running + couplings[mode_index] * ((bose_factor[mode_index] + 1.0) * below_shift + bose_factor[mode_index] * above_shift)
    return running


def reference(hamiltonian, coupling, sigma_old, orbital_coupling, momentum_weights, bose_factor, shifts):
    energies = -1.0 + 2.0 * jnp.arange(E_ALL, dtype=jnp.float32) / E_ALL

    def one_point(point_index):
        energy_index = point_index // K_ALL
        momentum_index = point_index % K_ALL
        local_ham = hamiltonian[momentum_index]
        local_link = coupling[momentum_index]
        local_sigma = sigma_old[energy_index, momentum_index]
        herm_real, herm_imag = hermitian_part(local_ham[0], local_ham[1])
        return green_blocks(herm_real, herm_imag, local_link[0], local_link[1], local_sigma[0], local_sigma[1], energies[energy_index])

    greens = lax.map(one_point, jnp.arange(E_ALL * K_ALL, dtype=jnp.int32))
    greens = greens.reshape(E_ALL, K_ALL, 2 * SLABS * B * B)
    momentum_mix = jnp.einsum("kq,eqx->ekx", momentum_weights, greens, precision=lax.Precision.HIGHEST) / K_ALL
    padded = jnp.pad(momentum_mix, ((SHIFT_MAX, SHIFT_MAX), (0, 0), (0, 0)))
    return phonon_sum(padded, E_ALL, orbital_coupling, bose_factor, shifts, (E_ALL, K_ALL, 2, SLABS, B, B))
```

```python
import functools

import jax
import jax.numpy as jnp
from jax import lax
from jax.experimental import pallas as pl
from jax.experimental.pallas import tpu as pltpu
from jax.sharding import PartitionSpec as P

BROADENING = 0.05
VMEM_LIMIT = 40 * 2**20
BF16 = jnp.bfloat16
F32 = jnp.float32


def split(x):
    high = x.astype(BF16)
    return high, (x - high.astype(F32)).astype(BF16)


def dot(a, b):
    return jnp.dot(a, b, preferred_element_type=F32)


def product(a, b):
    return dot(a[0], b[0]) + (dot(a[0], b[1]) + dot(a[1], b[0]))


def halves(pair):
    real, imag = pair
    return split(real), split(imag), split(real + imag)


def complex_product(a, b):
    rr = product(a[0], b[0])
    ii = product(a[1], b[1])
    both = product(a[2], b[2])
    return rr - ii, both - (rr + ii)


def reciprocal(real, imag):
    scale = 1.0 / (real * real + imag * imag)
    return real * scale, -imag * scale


def newton_inverse(ar, ai, eye):
    dr, di = jnp.where(eye, ar, 0.0), jnp.where(eye, ai, 0.0)
    row_r, row_i = reciprocal(jnp.sum(dr, 0, keepdims=True), jnp.sum(di, 0, keepdims=True))
    col_r, col_i = reciprocal(jnp.sum(dr, 1, keepdims=True), jnp.sum(di, 1, keepdims=True))
    nr = jnp.where(eye, 0.0, ar * row_r - ai * row_i)
    ni = jnp.where(eye, 0.0, ar * row_i + ai * row_r)
    n = halves((nr, ni))
    second = complex_product(n, n)
    n2 = halves(second)
    third = complex_product(n2, n)
    fourth = complex_product(n2, n2)
    qr = jnp.where(eye, 1.0, 0.0) - nr + second[0] - third[0]
    qi = second[1] - ni - third[1]
    tail = complex_product(halves((qr, qi)), halves(fourth))
    sr, si = qr + tail[0], qi + tail[1]
    return col_r * sr - col_i * si, col_r * si + col_i * sr


def greens_kernel(energy, z_ref, ham, link, sigma, last_ref, rest_ref, hbuf, tbuf, sbuf, sems):
    slabs, b = hbuf.shape[1], hbuf.shape[-1]
    copies = []
    for s in range(slabs):
        copies.append(pltpu.make_async_copy(ham.at[:, s], hbuf.at[:, s], sems.at[s]))
        copies.append(pltpu.make_async_copy(sigma.at[energy, :, s], sbuf.at[:, s], sems.at[slabs + s]))
        if s + 1 < slabs:
            copies.append(pltpu.make_async_copy(link.at[:, s], tbuf.at[:, s], sems.at[2 * slabs + s]))
    for copy in copies:
        copy.start()
    eye = lax.broadcasted_iota(jnp.int32, (b, b), 0) == lax.broadcasted_iota(jnp.int32, (b, b), 1)
    z = z_ref[energy]
    forward, adjoint_side, outward = [], [], []
    for s in range(slabs):
        copies[3 * s].wait()
        copies[3 * s + 1].wait()
        ar = jnp.where(eye, z, 0.0) - 0.5 * (hbuf[0, s] + hbuf[0, s].T) - sbuf[0, s]
        ai = jnp.where(eye, BROADENING, 0.0) - 0.5 * (hbuf[1, s] - hbuf[1, s].T) - sbuf[1, s]
        if s > 0:
            copies[3 * s - 1].wait()
            tr, ti = tbuf[0, s - 1], tbuf[1, s - 1]
            t_halves = halves((tr, ti))
            g_halves = halves(forward[-1])
            leaving = halves(complex_product(halves((tr.T, -ti.T)), g_halves))
            folded = complex_product(leaving, t_halves)
            ar, ai = ar - folded[0], ai - folded[1]
            adjoint_side.append(leaving)
            outward.append(halves(complex_product(g_halves, t_halves)))
        forward.append(newton_inverse(ar, ai, eye))
    block = forward[-1]
    last_ref[0], last_ref[1] = block
    for s in range(slabs - 2, -1, -1):
        through = halves(complex_product(outward[s], halves(block)))
        closing = complex_product(through, adjoint_side[s])
        block = (forward[s][0] + closing[0], forward[s][1] + closing[1])
        rest_ref[0, s], rest_ref[1, s] = block


def greens(energy, z, ham, link, sigma):
    _, slabs, b, _ = ham.shape
    hbm = pl.BlockSpec(memory_space=pltpu.HBM)
    vmem = pl.BlockSpec(memory_space=pltpu.VMEM)
    return pl.pallas_call(
        functools.partial(greens_kernel, energy),
        out_shape=[
            jax.ShapeDtypeStruct((2, b, b), F32),
            jax.ShapeDtypeStruct((2, slabs - 1, b, b), F32),
        ],
        in_specs=[pl.BlockSpec(memory_space=pltpu.SMEM), hbm, hbm, hbm],
        out_specs=[vmem, vmem],
        scratch_shapes=[
            pltpu.VMEM((2, slabs, b, b), F32),
            pltpu.VMEM((2, slabs - 1, b, b), F32),
            pltpu.VMEM((2, slabs, b, b), F32),
            pltpu.SemaphoreType.DMA((3 * slabs - 1,)),
        ],
        compiler_params=pltpu.CompilerParams(vmem_limit_bytes=VMEM_LIMIT),
        cost_estimate=pl.CostEstimate(flops=8 * 10**9, bytes_accessed=4 * 10**6, transcendentals=0),
    )(z, ham, link, sigma)


def swap_pairs(x, axis):
    return lax.ppermute(x, axis, [(i, i ^ 1) for i in range(lax.axis_size(axis))])


def shift_groups(x, axis, step):
    n = lax.axis_size(axis)
    return lax.ppermute(x, axis, [(i, (i + 2 * step) % n) for i in range(n)])


def pass_on(x, axis):
    n = lax.axis_size(axis)
    up = [(i, i + 2) for i in range(0, n - 2, 2)]
    down = [(i, i - 2) for i in range(3, n, 2)]
    return lax.ppermute(x, axis, up + down)


def body(hamiltonian, coupling, sigma_old, orbital_coupling, momentum_weights, bose_factor, shifts):
    k_all, e_dev = lax.axis_size("mom"), sigma_old.shape[0]
    groups = k_all // 2
    e_all = e_dev * lax.axis_size("energy")
    e_at, k_at = lax.axis_index("energy"), lax.axis_index("mom")
    odd = (e_at % 2) == 1
    weights = momentum_weights / k_all
    energies = -1.0 + 2.0 * (e_at * e_dev + jnp.arange(e_dev, dtype=jnp.int32)).astype(F32) / e_all

    def weight(k, q):
        return weights[k % k_all, q % k_all]

    def factor(shift, occupation):
        chosen = jnp.where(shifts == shift, occupation, 0.0)
        return sum(chosen[m] * orbital_coupling[m] for m in range(shifts.shape[0]))

    down1, down2 = factor(1, bose_factor + 1.0), factor(2, bose_factor + 1.0)
    up1, up2 = factor(1, bose_factor), factor(2, bose_factor)

    def neighbours(swapped, passed):
        return (
            [jnp.where(odd, s, p) for s, p in zip(swapped, passed)],
            [jnp.where(odd, p, s) for s, p in zip(swapped, passed)],
        )

    def phonons(own, swapped, passed):
        before, after = neighbours(swapped, passed)
        return (
            down1 * before[1] + down2 * before[0] + up1 * own[1] + up2 * after[0],
            down1 * own[0] + down2 * before[1] + up1 * after[0] + up2 * after[1],
        )

    def mix_gathered(x):
        held = [(k_at, x)]
        for j in range(1, groups):
            held.append((k_at - 2 * j + k_all, shift_groups(x, "mom", j)))
        partner = k_at ^ 1
        mine = sum(weight(k_at, q) * v for q, v in held)
        other = sum(weight(partner, q) * v for q, v in held)
        return mine + swap_pairs(other, "mom")

    def mix_paired(x):
        mate = swap_pairs(x, "mom")
        partner = k_at ^ 1
        total = weight(k_at, k_at) * x + weight(k_at, partner) * mate
        for j in range(1, groups):
            k = k_at + 2 * j
            total = total + shift_groups(weight(k, k_at) * x + weight(k, partner) * mate, "mom", j)
        return total

    last, rest = [], []
    for e in range(e_dev):
        l, r = greens(e, energies, hamiltonian[0], coupling[0], sigma_old[:, 0])
        last.append(l)
        rest.append(r)
    last_swapped = [swap_pairs(x, "energy") for x in last]
    last_passed = pass_on(jnp.stack(last_swapped), "energy")
    last_sum = jnp.stack(phonons(last, last_swapped, last_passed))
    last_out = mix_paired(last_sum)
    rest_mixed = [mix_gathered(x) for x in rest]
    rest_swapped = [swap_pairs(x, "energy") for x in rest_mixed]
    rest_passed = [pass_on(x, "energy") for x in rest_swapped]
    rest_out = jnp.stack(phonons(rest_mixed, rest_swapped, rest_passed))
    return jnp.concatenate([rest_out, last_out[:, :, None]], axis=2)[:, None]


def solution(mesh):
    return jax.shard_map(
        body,
        mesh=mesh,
        in_specs=(
            P("mom", None, None, None, None),
            P("mom", None, None, None, None),
            P("energy", "mom", None, None, None, None),
            P(),
            P(),
            P(),
            P(),
        ),
        out_specs=P("energy", "mom", None, None, None, None),
        check_vma=False,
    )
```

```python
import functools

import jax
import jax.numpy as jnp
import numpy as np
from jax import lax
from jax.experimental import pallas as pl
from jax.experimental.pallas import tpu as pltpu
from jax.sharding import PartitionSpec as P

BROADENING = 0.05
GREENS_VMEM = 56 * 2**20
POINT_VMEM = 24 * 2**20
ROWS = 8
LANES = 128
PIECES = 2
BF16 = jnp.bfloat16
F32 = jnp.float32


def split(x):
    high = x.astype(BF16)
    return high, (x - high.astype(F32)).astype(BF16)


def dot(a, b):
    return jnp.dot(a, b, preferred_element_type=F32)


def product(a, b):
    return dot(a[0], b[0]) + (dot(a[0], b[1]) + dot(a[1], b[0]))


def halves(pair):
    real, imag = pair
    return split(real), split(imag), split(real + imag)


def complex_product(a, b):
    rr = product(a[0], b[0])
    ii = product(a[1], b[1])
    both = product(a[2], b[2])
    return rr - ii, both - (rr + ii)


def reciprocal(real, imag):
    scale = 1.0 / (real * real + imag * imag)
    return real * scale, -imag * scale


def newton_inverse(ar, ai, eye):
    dr, di = jnp.where(eye, ar, 0.0), jnp.where(eye, ai, 0.0)
    row_r, row_i = reciprocal(jnp.sum(dr, 0, keepdims=True), jnp.sum(di, 0, keepdims=True))
    col_r, col_i = reciprocal(jnp.sum(dr, 1, keepdims=True), jnp.sum(di, 1, keepdims=True))
    nr = jnp.where(eye, 0.0, ar * row_r - ai * row_i)
    ni = jnp.where(eye, 0.0, ar * row_i + ai * row_r)
    n = halves((nr, ni))
    second = complex_product(n, n)
    n2 = halves(second)
    third = complex_product(n2, n)
    fourth = complex_product(n2, n2)
    qr = jnp.where(eye, 1.0, 0.0) - nr + second[0] - third[0]
    qi = second[1] - ni - third[1]
    tail = complex_product(halves((qr, qi)), halves(fourth))
    sr, si = qr + tail[0], qi + tail[1]
    return col_r * sr - col_i * si, col_r * si + col_i * sr


def pack(real, imag):
    width = real.shape[-1]
    full = width - width % LANES
    planes = [x[..., at : at + LANES] for x in (real, imag) for at in range(0, full, LANES)]
    if width > full:
        planes.append(jnp.concatenate([real[..., full:], imag[..., full:]], axis=-1))
    return planes


def unpack(planes, width):
    full = width - width % LANES
    each = full // LANES
    parts = [[(at * LANES, planes[p * each + at]) for at in range(each)] for p in range(2)]
    if width > full:
        rest = width - full
        parts[0].append((full, planes[-1][..., :rest]))
        parts[1].append((full, planes[-1][..., rest:]))
    return parts


def place(early, late, at, block):
    first, size = early.shape[1], block[0].shape[0]
    cut = min(max(first - at, 0), size)
    for plane, value in enumerate(pack(*block)):
        if cut > 0:
            early[plane, at : at + cut] = value[:cut]
        if cut < size:
            start = max(at - first, 0)
            late[plane, start : start + size - cut] = value[cut:]


def greens_kernel(energy, n_energy, _, ham, link, sigma, early, late, hbuf, tbuf, sbuf, sems):
    slabs, b = hbuf.shape[1], hbuf.shape[-1]
    copies = []
    for s in range(slabs):
        copies.append(pltpu.make_async_copy(ham.at[:, s], hbuf.at[:, s], sems.at[s]))
        copies.append(pltpu.make_async_copy(sigma.at[energy, :, s], sbuf.at[:, s], sems.at[slabs + s]))
        if s + 1 < slabs:
            copies.append(pltpu.make_async_copy(link.at[:, s], tbuf.at[:, s], sems.at[2 * slabs + s]))
    for copy in copies:
        copy.start()
    eye = lax.broadcasted_iota(jnp.int32, (b, b), 0) == lax.broadcasted_iota(jnp.int32, (b, b), 1)
    e_dev = sigma.shape[0]
    at = (lax.axis_index("energy") * e_dev + energy).astype(F32)
    z = -1.0 + jnp.full((1, 1), 2.0 * at, F32) / (e_dev * n_energy)
    forward, adjoint_side, outward = [], [], []
    for s in range(slabs):
        copies[3 * s].wait()
        copies[3 * s + 1].wait()
        ar = jnp.where(eye, z, 0.0) - 0.5 * (hbuf[0, s] + hbuf[0, s].T) - sbuf[0, s]
        ai = jnp.where(eye, BROADENING, 0.0) - 0.5 * (hbuf[1, s] - hbuf[1, s].T) - sbuf[1, s]
        if s > 0:
            copies[3 * s - 1].wait()
            tr, ti = tbuf[0, s - 1], tbuf[1, s - 1]
            t_halves = halves((tr, ti))
            g_halves = halves(forward[-1])
            leaving = halves(complex_product(halves((tr.T, -ti.T)), g_halves))
            folded = complex_product(leaving, t_halves)
            ar, ai = ar - folded[0], ai - folded[1]
            adjoint_side.append(leaving)
            outward.append(halves(complex_product(g_halves, t_halves)))
        forward.append(newton_inverse(ar, ai, eye))
    block = forward[-1]
    place(early, late, (slabs - 1) * b, block)
    for s in range(slabs - 2, -1, -1):
        through = halves(complex_product(outward[s], halves(block)))
        closing = complex_product(through, adjoint_side[s])
        block = (forward[s][0] + closing[0], forward[s][1] + closing[1])
        place(early, late, s * b, block)


HBM = pl.BlockSpec(memory_space=pltpu.HBM)
VMEM = pl.BlockSpec(memory_space=pltpu.VMEM)
SMEM = pl.BlockSpec(memory_space=pltpu.SMEM)
CHEAP = pl.CostEstimate(flops=0, bytes_accessed=0, transcendentals=0)


def greens(energy, n_energy, earlier, ham, link, sigma, late_rows):
    _, slabs, b, _ = ham.shape
    return pl.pallas_call(
        functools.partial(greens_kernel, energy, n_energy),
        out_shape=[
            jax.ShapeDtypeStruct((2 * b // LANES, slabs * b - late_rows, LANES), F32),
            jax.ShapeDtypeStruct((2 * b // LANES, late_rows, LANES), F32),
        ],
        in_specs=[pl.BlockSpec(memory_space=pl.ANY), HBM, HBM, HBM],
        out_specs=[VMEM, VMEM],
        scratch_shapes=[
            pltpu.VMEM((2, slabs, b, b), F32),
            pltpu.VMEM((2, slabs - 1, b, b), F32),
            pltpu.VMEM((2, slabs, b, b), F32),
            pltpu.SemaphoreType.DMA((3 * slabs - 1,)),
        ],
        compiler_params=pltpu.CompilerParams(vmem_limit_bytes=GREENS_VMEM),
        cost_estimate=pl.CostEstimate(flops=10**11, bytes_accessed=4 * 10**6, transcendentals=0),
    )(earlier, ham, link, sigma)


def row_loop(rows, step):
    def one(i, carry):
        step(pl.multiple_of(i * ROWS, ROWS))
        return carry

    lax.fori_loop(0, rows // ROWS, one, 0, unroll=2)


ANY = pl.BlockSpec(memory_space=pl.ANY)


def after(earlier, kernel):
    return lambda *refs: kernel(*refs[len(earlier) :])


def pointwise(earlier, kernel, shapes, specs, *args):
    return list(
        pl.pallas_call(
            after(earlier, kernel),
            out_shape=[jax.ShapeDtypeStruct(s, F32) for s in shapes],
            in_specs=[ANY] * len(earlier) + specs,
            out_specs=[VMEM] * len(shapes),
            compiler_params=pltpu.CompilerParams(vmem_limit_bytes=POINT_VMEM),
            cost_estimate=CHEAP,
        )(*earlier, *args)
    )


def weighted(out, terms):
    lead = out.shape[:-2]

    def step(at):
        rows = pl.ds(at, ROWS)
        for index in np.ndindex(*lead):
            total = None
            for scale, ref in terms:
                value = ref[(*index, rows)]
                value = value if scale is None else scale * value
                total = value if total is None else total + value
            out[(*index, rows)] = total

    row_loop(out.shape[-2], step)


def gathered_kernel(k_all, w, *refs):
    groups = k_all // 2
    held, mine, other = refs[:groups], refs[groups], refs[groups + 1 :]
    k = lax.axis_index("mom")
    each = mine.shape[0] // len(other)
    for i, out in enumerate((mine, *other)):
        to = k if i == 0 else k ^ 1
        terms = []
        for j, ref in enumerate(held):
            q = lax.rem(k - 2 * j + k_all, k_all)
            terms.append((w[to, q] / k_all, ref if i == 0 else ref.at[pl.ds((i - 1) * each, each)]))
        weighted(out, terms)


def paired_kernel(k_all, planes, w, *refs):
    xs, mates, outs = refs[:planes], refs[planes : 2 * planes], refs[2 * planes :]
    k = lax.axis_index("mom")
    for j, out in enumerate(outs):
        to = lax.rem(k + 2 * j, k_all)
        for plane in range(planes):
            weighted(out.at[:, plane], [(w[to, k] / k_all, xs[plane]), (w[to, k ^ 1] / k_all, mates[plane])])


def sum_kernel(x, *refs):
    outs = refs[-PIECES:]
    arrived = refs[:-PIECES]
    each, rows = arrived[0].shape[0], outs[0].shape[1]
    for piece, out in enumerate(outs):
        here = pl.ds(piece * rows, rows)
        for i, y in enumerate(arrived):
            planes = pl.ds(i * each, each)
            weighted(out.at[planes], [(None, x.at[planes, here]), (None, y.at[:, here])])


def phonon_rows(first_row, n_energy, b, shifts, bose, orbital, own, swapped, passed, write):
    modes, planes = orbital.shape[0], own[0].shape[0]
    e = lax.axis_index("energy")
    odd = lax.rem(e, 2) == 1
    edge = jnp.logical_or(e == 0, e == n_energy - 1)
    zero = jnp.float32(0.0)

    def scales(shift, down, up):
        out = []
        for m in range(modes):
            hit = shifts[m] == shift
            below = jnp.where(jnp.logical_and(hit, down), bose[m] + 1.0, zero)
            above = jnp.where(jnp.logical_and(hit, up), bose[m], zero)
            out.append(below + above)
        return out

    even = jnp.logical_not(odd)
    inner = jnp.logical_not(edge)
    lower, upper = jnp.logical_and(even, inner), jnp.logical_and(odd, inner)
    always, never = e >= 0, e < 0
    tables = [
        scales(1, always, never),
        scales(1, never, always),
        scales(2, odd, even),
        scales(1, odd, never),
        scales(1, never, even),
        scales(2, lower, upper),
        scales(1, lower, never),
        scales(1, never, upper),
    ]
    full = b // LANES

    def step(at):
        rows = pl.ds(at, ROWS)
        orbit = pl.ds(pl.multiple_of(lax.rem(at + first_row, b), ROWS), ROWS)
        for column in range(orbital.shape[1]):
            modes_here = [orbital[m, column, orbit] for m in range(modes)]
            down1, up1, s2, s1_low, s1_high, p2, p1_low, p1_high = [
                sum(s * v for s, v in zip(table, modes_here)) for table in tables
            ]
            for plane in [column, full + column] if column < full else [planes - 1]:
                oa, ob = own[0][plane, rows], own[1][plane, rows]
                sa, sb = swapped[0][plane, rows], swapped[1][plane, rows]
                pa, pb = passed[0][plane, rows], passed[1][plane, rows]
                write(0, plane, at, up1 * ob + s2 * sa + s1_low * sb + p2 * pa + p1_low * pb)
                write(1, plane, at, down1 * oa + s2 * sb + s1_high * sa + p2 * pb + p1_high * pa)

    row_loop(own[0].shape[1], step)


def late_phonon_kernel(first_row, n_energy, b, shifts, bose, orbital, oa, ob, sa, sb, pa, pb, *outs):
    def write(energy, plane, at, value):
        outs[plane][energy, pl.ds(at, ROWS)] = value

    phonon_rows(first_row, n_energy, b, shifts, bose, orbital, [oa, ob], [sa, sb], [pa, pb], write)


def store_unpacked(held, energy, at, planes):
    width = held.shape[-1]
    for part, pieces in enumerate(unpack(planes, width)):
        for lane, value in pieces:
            held[energy, part, pl.ds(at, ROWS), lane : lane + value.shape[-1]] = value


def late_out_kernel(first_row, groups, total, *refs):
    arrived = refs[: groups - 1]
    out, held, sem = refs[-3:]
    energies, planes, rows, _ = total.shape

    def step(at):
        here = pl.ds(at, ROWS)
        for energy in range(energies):
            values = []
            for plane in range(planes):
                value = total[energy, plane, here]
                for ref in arrived:
                    value = value + ref[energy, plane, here]
                values.append(value)
            store_unpacked(held, energy, at, values)

    row_loop(rows, step)
    copy = pltpu.make_async_copy(held, out.at[:, :, pl.ds(first_row, rows)], sem)
    copy.start()
    copy.wait()


def early_out_kernel(n_energy, first_row, shifts, bose, orbital, oa, sa, pa, ob, sb, pb, *refs):
    out, held, sem = refs[-3:]
    rows, b = held.shape[2:]
    planes = oa.shape[0]
    got = {}

    def write(energy, plane, at, value):
        got[energy, plane] = value
        if plane == planes - 1:
            store_unpacked(held, energy, at, [got[energy, p] for p in range(planes)])

    phonon_rows(first_row, n_energy, b, shifts, bose, orbital, [oa, ob], [sa, sb], [pa, pb], write)
    copy = pltpu.make_async_copy(held, out.at[:, :, pl.ds(first_row, rows)], sem)
    copy.start()
    copy.wait()


def swap_pairs(x, axis):
    return lax.ppermute(x, axis, [(i, i ^ 1) for i in range(lax.axis_size(axis))])


def shift_groups(x, axis, step):
    n = lax.axis_size(axis)
    return lax.ppermute(x, axis, [(i, (i + 2 * step) % n) for i in range(n)])


def pass_on(x, axis):
    n = lax.axis_size(axis)
    return lax.ppermute(x, axis, [(i, (i + (2 if i % 2 == 0 else n - 2)) % n) for i in range(n)])


def body(hamiltonian, coupling, sigma_old, orbital_coupling, momentum_weights, bose_factor, shifts):
    k_all, n_energy = lax.axis_size("mom"), lax.axis_size("energy")
    e_dev, _, _, slabs, b, _ = sigma_old.shape
    groups = k_all // 2
    late_rows = b + b // 4
    early_rows = slabs * b - late_rows

    early, late = [], []
    earlier = momentum_weights
    for e in range(e_dev):
        r, l = greens(e, n_energy, earlier, hamiltonian[0], coupling[0], sigma_old[:, 0], late_rows)
        early.append(r)
        late.append(l)
        earlier = l

    full = b - b % LANES
    columns = [orbital_coupling[..., at : at + LANES] for at in range(0, full, LANES)]
    if full < b:
        columns.append(jnp.concatenate([orbital_coupling[..., full:]] * 2, axis=-1))
    orbital = jnp.stack(columns, axis=1)

    late_shape = (e_dev, *late[0].shape)
    planes, rows, lanes = early[0].shape

    def then(x, *earlier):
        return lax.optimization_barrier((x, *earlier))[0]

    def collect(x):
        return [x] + [shift_groups(x, "mom", j) for j in range(1, groups)]

    def gather(earlier, held):
        x = held[0]
        mine, *other = pointwise(
            earlier, functools.partial(gathered_kernel, k_all),
            [x.shape] + [(1, *x.shape[1:])] * planes,
            [SMEM] + [VMEM] * groups, momentum_weights, *held,
        )
        return mine, other

    def add_mate(earlier, mine, other):
        from_mate = [swap_pairs(x, "mom") for x in other]
        shapes = [(planes, rows // PIECES, lanes)] * PIECES
        return pointwise(earlier, sum_kernel, shapes, [VMEM] * (1 + len(other)), mine, *from_mate)

    late_swapped = [swap_pairs(late[0], "energy")]
    late_swapped.append(swap_pairs(then(late[1], late_swapped[0]), "energy"))
    late_passed = [pass_on(x, "energy") for x in late_swapped]
    held_a = collect(early[0])
    held_b = collect(then(early[1], *held_a[1:]))

    mine_a, other_a = gather([early[1]], held_a)
    mixed_a = add_mate([mine_a], mine_a, other_a)
    swapped_a = [swap_pairs(then(x, late_swapped[1]), "energy") for x in mixed_a]
    passed_a = [pass_on(x, "energy") for x in swapped_a]
    mine_b, other_b = gather([mixed_a[0], swapped_a[0], late_passed[0]], held_b)
    mixed_b = add_mate([mine_b, swapped_a[1]], mine_b, other_b)
    swapped_b = [swap_pairs(x, "energy") for x in mixed_b]
    passed_b = [pass_on(x, "energy") for x in swapped_b]
    late_sum = pointwise(
        [mixed_b[0]], functools.partial(late_phonon_kernel, early_rows, n_energy, b),
        [(e_dev, late_rows, lanes)] * planes, [SMEM, SMEM] + [VMEM] * 7,
        shifts, bose_factor, orbital, *late, *late_swapped, *late_passed,
    )
    mate = [swap_pairs(x, "mom") for x in late_sum]
    total, *sends = pointwise(
        [], functools.partial(paired_kernel, k_all, planes),
        [late_shape] * groups, [SMEM] + [VMEM] * (2 * planes), momentum_weights, *late_sum, *mate,
    )
    arrived = [shift_groups(x, "mom", j + 1) for j, x in enumerate(sends)]

    whole = (e_dev, 2, slabs * b, b)
    def write_out(kernel, rows, operands, specs, out=None):
        given = [] if out is None else [out]
        return pl.pallas_call(
            kernel,
            out_shape=jax.ShapeDtypeStruct(whole, F32),
            in_specs=specs + [HBM] * len(given),
            out_specs=HBM,
            scratch_shapes=[pltpu.VMEM((e_dev, 2, rows, b), F32), pltpu.SemaphoreType.DMA],
            input_output_aliases={len(operands): 0} if given else {},
            compiler_params=pltpu.CompilerParams(vmem_limit_bytes=POINT_VMEM),
            cost_estimate=CHEAP,
        )(*operands, *given)

    def early_out(i, out):
        operands = [shifts, bose_factor, orbital]
        operands += [x[i] for x in (mixed_a, swapped_a, passed_a, mixed_b, swapped_b, passed_b)]
        kernel = functools.partial(early_out_kernel, n_energy, i * (rows // PIECES))
        return write_out(kernel, rows // PIECES, operands, [SMEM, SMEM] + [VMEM] * 7, out)

    out = None
    for i in range(PIECES - 1):
        out = early_out(i, out)
    late_kernel = functools.partial(late_out_kernel, early_rows, groups)
    out = write_out(late_kernel, late_rows, [total, *arrived], [VMEM] * groups, out)
    out = early_out(PIECES - 1, out)
    return out.reshape(e_dev, 1, 2, slabs, b, b)


def solution(mesh):
    return jax.shard_map(
        body,
        mesh=mesh,
        in_specs=(
            P("mom", None, None, None, None),
            P("mom", None, None, None, None),
            P("energy", "mom", None, None, None, None),
            P(),
            P(),
            P(),
            P(),
        ),
        out_specs=P("energy", "mom", None, None, None, None),
        check_vma=False,
    )
```

```python
import functools

import jax
import jax.numpy as jnp
import numpy as np
from jax import lax
from jax.experimental import pallas as pl
from jax.experimental.pallas import tpu as pltpu
from jax.sharding import PartitionSpec as P

BROADENING = 0.05
GREENS_VMEM = 52 * 2**20
POINT_VMEM = 24 * 2**20
ROWS = 8
LANES = 128
PIECES = 2
UNROLL = 6
BF16 = jnp.bfloat16
F32 = jnp.float32


def split(x):
    high = x.astype(BF16)
    return high, (x - high.astype(F32)).astype(BF16)


def dot(a, b):
    return jnp.dot(a, b, preferred_element_type=F32)


def product(a, b):
    return dot(a[0], b[0]) + (dot(a[0], b[1]) + dot(a[1], b[0]))


def halves(pair):
    real, imag = pair
    return split(real), split(imag), split(real + imag)


def complex_product(a, b):
    rr = product(a[0], b[0])
    ii = product(a[1], b[1])
    both = product(a[2], b[2])
    return rr - ii, both - (rr + ii)


def reciprocal(real, imag):
    scale = 1.0 / (real * real + imag * imag)
    return real * scale, -imag * scale


def newton_inverse(ar, ai, eye):
    dr, di = jnp.where(eye, ar, 0.0), jnp.where(eye, ai, 0.0)
    row_r, row_i = reciprocal(jnp.sum(dr, 0, keepdims=True), jnp.sum(di, 0, keepdims=True))
    col_r, col_i = reciprocal(jnp.sum(dr, 1, keepdims=True), jnp.sum(di, 1, keepdims=True))
    nr = jnp.where(eye, 0.0, ar * row_r - ai * row_i)
    ni = jnp.where(eye, 0.0, ar * row_i + ai * row_r)
    n = halves((nr, ni))
    second = complex_product(n, n)
    n2 = halves(second)
    third = complex_product(n2, n)
    fourth = complex_product(n2, n2)
    qr = jnp.where(eye, 1.0, 0.0) - nr + second[0] - third[0]
    qi = second[1] - ni - third[1]
    tail = complex_product(halves((qr, qi)), halves(fourth))
    sr, si = qr + tail[0], qi + tail[1]
    return col_r * sr - col_i * si, col_r * si + col_i * sr


def pack(real, imag):
    width = real.shape[-1]
    full = width - width % LANES
    planes = [x[..., at : at + LANES] for x in (real, imag) for at in range(0, full, LANES)]
    if width > full:
        planes.append(jnp.concatenate([real[..., full:], imag[..., full:]], axis=-1))
    return planes


def unpack(planes, width):
    full = width - width % LANES
    each = full // LANES
    parts = [[(at * LANES, planes[p * each + at]) for at in range(each)] for p in range(2)]
    if width > full:
        rest = width - full
        parts[0].append((full, planes[-1][..., :rest]))
        parts[1].append((full, planes[-1][..., rest:]))
    return parts


def place(early, late, at, block):
    first, size = early.shape[1], block[0].shape[0]
    cut = min(max(first - at, 0), size)
    for plane, value in enumerate(pack(*block)):
        if cut > 0:
            early[plane, at : at + cut] = value[:cut]
        if cut < size:
            start = max(at - first, 0)
            late[plane, start : start + size - cut] = value[cut:]


def greens_kernel(energy, n_energy, _, ham, link, sigma, early, late, hbuf, tbuf, sbuf, sems):
    slabs, b = hbuf.shape[1], hbuf.shape[-1]
    copies = []
    for s in range(slabs):
        copies.append(pltpu.make_async_copy(ham.at[:, s], hbuf.at[:, s], sems.at[s]))
        copies.append(pltpu.make_async_copy(sigma.at[energy, :, s], sbuf.at[:, s], sems.at[slabs + s]))
        if s + 1 < slabs:
            copies.append(pltpu.make_async_copy(link.at[:, s], tbuf.at[:, s], sems.at[2 * slabs + s]))
    for copy in copies:
        copy.start()
    eye = lax.broadcasted_iota(jnp.int32, (b, b), 0) == lax.broadcasted_iota(jnp.int32, (b, b), 1)
    e_dev = sigma.shape[0]
    at = (lax.axis_index("energy") * e_dev + energy).astype(F32)
    z = -1.0 + jnp.full((1, 1), 2.0 * at, F32) / (e_dev * n_energy)
    forward, adjoint_side, outward = [], [], []
    for s in range(slabs):
        copies[3 * s].wait()
        copies[3 * s + 1].wait()
        ar = jnp.where(eye, z, 0.0) - 0.5 * (hbuf[0, s] + hbuf[0, s].T) - sbuf[0, s]
        ai = jnp.where(eye, BROADENING, 0.0) - 0.5 * (hbuf[1, s] - hbuf[1, s].T) - sbuf[1, s]
        if s > 0:
            copies[3 * s - 1].wait()
            tr, ti = tbuf[0, s - 1], tbuf[1, s - 1]
            t_halves = halves((tr, ti))
            g_halves = halves(forward[-1])
            leaving = halves(complex_product(halves((tr.T, -ti.T)), g_halves))
            folded = complex_product(leaving, t_halves)
            ar, ai = ar - folded[0], ai - folded[1]
            adjoint_side.append(leaving)
            outward.append(halves(complex_product(g_halves, t_halves)))
        forward.append(newton_inverse(ar, ai, eye))
    block = forward[-1]
    place(early, late, (slabs - 1) * b, block)
    for s in range(slabs - 2, -1, -1):
        through = halves(complex_product(outward[s], halves(block)))
        closing = complex_product(through, adjoint_side[s])
        block = (forward[s][0] + closing[0], forward[s][1] + closing[1])
        place(early, late, s * b, block)


HBM = pl.BlockSpec(memory_space=pltpu.HBM)
VMEM = pl.BlockSpec(memory_space=pltpu.VMEM)
SMEM = pl.BlockSpec(memory_space=pltpu.SMEM)
CHEAP = pl.CostEstimate(flops=0, bytes_accessed=0, transcendentals=0)


def greens(energy, n_energy, earlier, ham, link, sigma, late_rows):
    _, slabs, b, _ = ham.shape
    return pl.pallas_call(
        functools.partial(greens_kernel, energy, n_energy),
        out_shape=[
            jax.ShapeDtypeStruct((2 * b // LANES, slabs * b - late_rows, LANES), F32),
            jax.ShapeDtypeStruct((2 * b // LANES, late_rows, LANES), F32),
        ],
        in_specs=[pl.BlockSpec(memory_space=pl.ANY), HBM, HBM, HBM],
        out_specs=[VMEM, VMEM],
        scratch_shapes=[
            pltpu.VMEM((2, slabs, b, b), F32),
            pltpu.VMEM((2, slabs - 1, b, b), F32),
            pltpu.VMEM((2, slabs, b, b), F32),
            pltpu.SemaphoreType.DMA((3 * slabs - 1,)),
        ],
        compiler_params=pltpu.CompilerParams(vmem_limit_bytes=GREENS_VMEM),
        cost_estimate=pl.CostEstimate(flops=10**11, bytes_accessed=4 * 10**6, transcendentals=0),
    )(earlier, ham, link, sigma)


def row_loop(rows, step):
    def one(i, carry):
        step(pl.multiple_of(i * ROWS, ROWS))
        return carry

    lax.fori_loop(0, rows // ROWS, one, 0, unroll=UNROLL)


ANY = pl.BlockSpec(memory_space=pl.ANY)


def after(earlier, kernel):
    return lambda *refs: kernel(*refs[len(earlier) :])


def pointwise(earlier, kernel, shapes, specs, *args):
    return list(
        pl.pallas_call(
            after(earlier, kernel),
            out_shape=[jax.ShapeDtypeStruct(s, F32) for s in shapes],
            in_specs=[ANY] * len(earlier) + specs,
            out_specs=[VMEM] * len(shapes),
            compiler_params=pltpu.CompilerParams(vmem_limit_bytes=POINT_VMEM),
            cost_estimate=CHEAP,
        )(*earlier, *args)
    )


def weighted(out, terms):
    lead = out.shape[:-2]

    def step(at):
        rows = pl.ds(at, ROWS)
        for index in np.ndindex(*lead):
            total = None
            for scale, ref in terms:
                value = ref[(*index, rows)]
                value = value if scale is None else scale * value
                total = value if total is None else total + value
            out[(*index, rows)] = total

    row_loop(out.shape[-2], step)


def gathered_kernel(k_all, w, *refs):
    groups = k_all // 2
    held, mine, other = refs[:groups], refs[groups], refs[groups + 1 :]
    k = lax.axis_index("mom")
    each = mine.shape[0] // len(other)
    for i, out in enumerate((mine, *other)):
        to = k if i == 0 else k ^ 1
        terms = []
        for j, ref in enumerate(held):
            q = lax.rem(k - 2 * j + k_all, k_all)
            terms.append((w[to, q] / k_all, ref if i == 0 else ref.at[pl.ds((i - 1) * each, each)]))
        weighted(out, terms)


def paired_kernel(k_all, planes, w, *refs):
    xs, mates, outs = refs[:planes], refs[planes : 2 * planes], refs[2 * planes :]
    k = lax.axis_index("mom")
    e_dev = xs[0].shape[0]
    for i, out in enumerate(outs):
        to = lax.rem(k + 2 * (i // e_dev), k_all)
        for plane in range(planes):
            x, mate = xs[plane].at[i % e_dev], mates[plane].at[i % e_dev]
            weighted(out.at[plane], [(w[to, k] / k_all, x), (w[to, k ^ 1] / k_all, mate)])


def sum_kernel(x, *refs):
    outs = refs[-PIECES:]
    arrived = refs[:-PIECES]
    each, rows = arrived[0].shape[0], outs[0].shape[1]
    for piece, out in enumerate(outs):
        here = pl.ds(piece * rows, rows)
        for i, y in enumerate(arrived):
            planes = pl.ds(i * each, each)
            weighted(out.at[planes], [(None, x.at[planes, here]), (None, y.at[:, here])])


def phonon_rows(first_row, n_energy, b, shifts, bose, orbital, own, swapped, passed, write):
    modes, planes = orbital.shape[0], own[0].shape[0]
    e = lax.axis_index("energy")
    odd = lax.rem(e, 2) == 1
    edge = jnp.logical_or(e == 0, e == n_energy - 1)
    zero = jnp.float32(0.0)

    def scales(shift, down, up):
        out = []
        for m in range(modes):
            hit = shifts[m] == shift
            below = jnp.where(jnp.logical_and(hit, down), bose[m] + 1.0, zero)
            above = jnp.where(jnp.logical_and(hit, up), bose[m], zero)
            out.append(below + above)
        return out

    even = jnp.logical_not(odd)
    inner = jnp.logical_not(edge)
    lower, upper = jnp.logical_and(even, inner), jnp.logical_and(odd, inner)
    always, never = e >= 0, e < 0
    tables = [
        scales(1, always, never),
        scales(1, never, always),
        scales(2, odd, even),
        scales(1, odd, never),
        scales(1, never, even),
        scales(2, lower, upper),
        scales(1, lower, never),
        scales(1, never, upper),
    ]
    full = b // LANES

    def step(at):
        rows = pl.ds(at, ROWS)
        orbit = pl.ds(pl.multiple_of(lax.rem(at + first_row, b), ROWS), ROWS)
        for column in range(orbital.shape[1]):
            modes_here = [orbital[m, column, orbit] for m in range(modes)]
            down1, up1, s2, s1_low, s1_high, p2, p1_low, p1_high = [
                sum(s * v for s, v in zip(table, modes_here)) for table in tables
            ]
            for plane in [column, full + column] if column < full else [planes - 1]:
                oa, ob = own[0][plane, rows], own[1][plane, rows]
                sa, sb = swapped[0][plane, rows], swapped[1][plane, rows]
                pa, pb = passed[0][plane, rows], passed[1][plane, rows]
                write(0, plane, at, up1 * ob + s2 * sa + s1_low * sb + p2 * pa + p1_low * pb)
                write(1, plane, at, down1 * oa + s2 * sb + s1_high * sa + p2 * pb + p1_high * pa)

    row_loop(own[0].shape[1], step)


def late_phonon_kernel(first_row, n_energy, b, shifts, bose, orbital, oa, ob, sa, sb, pa, pb, *outs):
    def write(energy, plane, at, value):
        outs[plane][energy, pl.ds(at, ROWS)] = value

    phonon_rows(first_row, n_energy, b, shifts, bose, orbital, [oa, ob], [sa, sb], [pa, pb], write)


def store_unpacked(held, energy, at, planes):
    width = held.shape[-1]
    for part, pieces in enumerate(unpack(planes, width)):
        for lane, value in pieces:
            held[energy, part, pl.ds(at, ROWS), lane : lane + value.shape[-1]] = value


def late_out_kernel(first_row, count, *refs):
    arrived = refs[:count]
    out, held, sem = refs[-3:]
    energies, (planes, rows, _) = held.shape[0], arrived[0].shape

    def step(at):
        here = pl.ds(at, ROWS)
        for energy in range(energies):
            values = []
            for plane in range(planes):
                values.append(sum(ref[plane, here] for ref in arrived[energy::energies]))
            store_unpacked(held, energy, at, values)

    row_loop(rows, step)
    copy = pltpu.make_async_copy(held, out.at[:, :, pl.ds(first_row, rows)], sem)
    copy.start()
    copy.wait()


def early_out_kernel(n_energy, first_row, shifts, bose, orbital, oa, sa, pa, ob, sb, pb, *refs):
    out, held, sem = refs[-3:]
    rows, b = held.shape[2:]
    planes = oa.shape[0]
    got = {}

    def write(energy, plane, at, value):
        got[energy, plane] = value
        if plane == planes - 1:
            store_unpacked(held, energy, at, [got[energy, p] for p in range(planes)])

    phonon_rows(first_row, n_energy, b, shifts, bose, orbital, [oa, ob], [sa, sb], [pa, pb], write)
    copy = pltpu.make_async_copy(held, out.at[:, :, pl.ds(first_row, rows)], sem)
    copy.start()
    copy.wait()


def swap_pairs(x, axis):
    return lax.ppermute(x, axis, [(i, i ^ 1) for i in range(lax.axis_size(axis))])


def shift_groups(x, axis, step):
    n = lax.axis_size(axis)
    return lax.ppermute(x, axis, [(i, (i + 2 * step) % n) for i in range(n)])


def pass_on(x, axis):
    n = lax.axis_size(axis)
    return lax.ppermute(x, axis, [(i, (i + (2 if i % 2 == 0 else n - 2)) % n) for i in range(n)])


def body(hamiltonian, coupling, sigma_old, orbital_coupling, momentum_weights, bose_factor, shifts):
    k_all, n_energy = lax.axis_size("mom"), lax.axis_size("energy")
    e_dev, _, _, slabs, b, _ = sigma_old.shape
    groups = k_all // 2
    late_rows = b + b // 4
    early_rows = slabs * b - late_rows

    early, late = [], []
    earlier = orbital_coupling
    for e in range(e_dev):
        r, l = greens(e, n_energy, earlier, hamiltonian[0], coupling[0], sigma_old[:, 0], late_rows)
        early.append(r)
        late.append(l)
        earlier = l

    full = b - b % LANES
    columns = [orbital_coupling[..., at : at + LANES] for at in range(0, full, LANES)]
    if full < b:
        columns.append(jnp.concatenate([orbital_coupling[..., full:]] * 2, axis=-1))
    orbital = jnp.stack(columns, axis=1)

    planes, rows, lanes = early[0].shape

    def then(x, *earlier):
        return lax.optimization_barrier((x, *earlier))[0]

    def collect(x):
        return [x] + [shift_groups(x, "mom", j) for j in range(1, groups)]

    def gather(earlier, held):
        x = held[0]
        mine, *other = pointwise(
            earlier, functools.partial(gathered_kernel, k_all),
            [x.shape] + [(1, *x.shape[1:])] * planes,
            [SMEM] + [VMEM] * groups, momentum_weights, *held,
        )
        return mine, other

    def add_mate(earlier, mine, other):
        from_mate = [swap_pairs(x, "mom") for x in other]
        shapes = [(planes, rows // PIECES, lanes)] * PIECES
        return pointwise(earlier, sum_kernel, shapes, [VMEM] * (1 + len(other)), mine, *from_mate)

    late_swapped = [swap_pairs(late[0], "energy")]
    late_swapped.append(swap_pairs(then(late[1], late_swapped[0]), "energy"))
    late_passed = [pass_on(x, "energy") for x in late_swapped]
    held_a = collect(early[0])
    held_b = collect(then(early[1], *held_a[1:]))

    mine_a, other_a = gather([early[1]], held_a)
    mixed_a = add_mate([mine_a], mine_a, other_a)
    swapped_a = [swap_pairs(then(x, late_swapped[1]), "energy") for x in mixed_a]
    passed_a = [pass_on(swapped_a[0], "energy")]
    for x in swapped_a[1:]:
        passed_a.append(pass_on(then(x, passed_a[-1]), "energy"))
    mine_b, other_b = gather([mixed_a[0], swapped_a[0], late_passed[0]], held_b)
    mixed_b = add_mate([mine_b, swapped_a[1]], mine_b, other_b)
    swapped_b = [swap_pairs(x, "energy") for x in mixed_b]
    passed_b = [pass_on(then(swapped_b[0], passed_a[-1]), "energy")]
    for x in swapped_b[1:]:
        passed_b.append(pass_on(x, "energy"))
    late_sum = pointwise(
        [mixed_b[0]], functools.partial(late_phonon_kernel, early_rows, n_energy, b),
        [(e_dev, late_rows, lanes)] * planes, [SMEM, SMEM] + [VMEM] * 7,
        shifts, bose_factor, orbital, *late, *late_swapped, *late_passed,
    )
    mate = [swap_pairs(x, "mom") for x in late_sum]
    sends = pointwise(
        [], functools.partial(paired_kernel, k_all, planes),
        [late[0].shape] * (groups * e_dev), [SMEM] + [VMEM] * (2 * planes), momentum_weights, *late_sum, *mate,
    )
    arrived = [x if i < e_dev else shift_groups(x, "mom", i // e_dev) for i, x in enumerate(sends)]

    whole = (e_dev, 2, slabs * b, b)
    def write_out(kernel, rows, operands, specs, out=None):
        given = [] if out is None else [out]
        return pl.pallas_call(
            kernel,
            out_shape=jax.ShapeDtypeStruct(whole, F32),
            in_specs=specs + [HBM] * len(given),
            out_specs=HBM,
            scratch_shapes=[pltpu.VMEM((e_dev, 2, rows, b), F32), pltpu.SemaphoreType.DMA],
            input_output_aliases={len(operands): 0} if given else {},
            compiler_params=pltpu.CompilerParams(vmem_limit_bytes=POINT_VMEM),
            cost_estimate=CHEAP,
        )(*operands, *given)

    def early_out(i, out):
        operands = [shifts, bose_factor, orbital]
        operands += [x[i] for x in (mixed_a, swapped_a, passed_a, mixed_b, swapped_b, passed_b)]
        kernel = functools.partial(early_out_kernel, n_energy, i * (rows // PIECES))
        return write_out(kernel, rows // PIECES, operands, [SMEM, SMEM] + [VMEM] * 7, out)

    out = None
    for i in range(PIECES - 1):
        out = early_out(i, out)
    late_kernel = functools.partial(late_out_kernel, early_rows, len(arrived))
    out = write_out(late_kernel, late_rows, arrived, [VMEM] * len(arrived), out)
    out = early_out(PIECES - 1, out)
    return out.reshape(e_dev, 1, 2, slabs, b, b)


def solution(mesh):
    return jax.shard_map(
        body,
        mesh=mesh,
        in_specs=(
            P("mom", None, None, None, None),
            P("mom", None, None, None, None),
            P("energy", "mom", None, None, None, None),
            P(),
            P(),
            P(),
            P(),
        ),
        out_specs=P("energy", "mom", None, None, None, None),
        check_vma=False,
    )
```

```python
import functools

import jax
import jax.numpy as jnp
import numpy as np
from jax import lax
from jax.experimental import pallas as pl
from jax.experimental.pallas import tpu as pltpu
from jax.sharding import PartitionSpec as P

BROADENING = 0.05
GREENS_VMEM = 52 * 2**20
POINT_VMEM = 24 * 2**20
ROWS = 8
LANES = 128
PIECES = 2
UNROLL = 6
BF16 = jnp.bfloat16
F32 = jnp.float32


def split(x):
    high = x.astype(BF16)
    return high, (x - high.astype(F32)).astype(BF16)


def dot(a, b):
    return jnp.dot(a, b, preferred_element_type=F32)


def product(a, b):
    return dot(a[0], b[0]) + (dot(a[0], b[1]) + dot(a[1], b[0]))


def halves(pair):
    real, imag = pair
    return split(real), split(imag), split(real + imag)


def complex_product(a, b):
    rr = product(a[0], b[0])
    ii = product(a[1], b[1])
    both = product(a[2], b[2])
    return rr - ii, both - (rr + ii)


def reciprocal(real, imag):
    scale = 1.0 / (real * real + imag * imag)
    return real * scale, -imag * scale


def newton_inverse(ar, ai, eye):
    dr, di = jnp.where(eye, ar, 0.0), jnp.where(eye, ai, 0.0)
    row_r, row_i = reciprocal(jnp.sum(dr, 0, keepdims=True), jnp.sum(di, 0, keepdims=True))
    col_r, col_i = reciprocal(jnp.sum(dr, 1, keepdims=True), jnp.sum(di, 1, keepdims=True))
    nr = jnp.where(eye, 0.0, ar * row_r - ai * row_i)
    ni = jnp.where(eye, 0.0, ar * row_i + ai * row_r)
    n = halves((nr, ni))
    second = complex_product(n, n)
    n2 = halves(second)
    third = complex_product(n2, n)
    fourth = complex_product(n2, n2)
    qr = jnp.where(eye, 1.0, 0.0) - nr + second[0] - third[0]
    qi = second[1] - ni - third[1]
    tail = complex_product(halves((qr, qi)), halves(fourth))
    sr, si = qr + tail[0], qi + tail[1]
    return col_r * sr - col_i * si, col_r * si + col_i * sr


def pack(real, imag):
    width = real.shape[-1]
    full = width - width % LANES
    planes = [x[..., at : at + LANES] for x in (real, imag) for at in range(0, full, LANES)]
    if width > full:
        planes.append(jnp.concatenate([real[..., full:], imag[..., full:]], axis=-1))
    return planes


def unpack(planes, width):
    full = width - width % LANES
    each = full // LANES
    parts = [[(at * LANES, planes[p * each + at]) for at in range(each)] for p in range(2)]
    if width > full:
        rest = width - full
        parts[0].append((full, planes[-1][..., :rest]))
        parts[1].append((full, planes[-1][..., rest:]))
    return parts


def place(early, late, at, block):
    first, size = early.shape[1], block[0].shape[0]
    cut = min(max(first - at, 0), size)
    for plane, value in enumerate(pack(*block)):
        if cut > 0:
            early[plane, at : at + cut] = value[:cut]
        if cut < size:
            start = max(at - first, 0)
            late[plane, start : start + size - cut] = value[cut:]


def greens_kernel(energy, n_energy, ham, link, sigma, early, late, hbuf, tbuf, sbuf, sems):
    slabs, b = hbuf.shape[1], hbuf.shape[-1]
    copies = []
    for s in range(slabs):
        copies.append(pltpu.make_async_copy(ham.at[:, s], hbuf.at[:, s], sems.at[s]))
        copies.append(pltpu.make_async_copy(sigma.at[energy, :, s], sbuf.at[:, s], sems.at[slabs + s]))
        if s + 1 < slabs:
            copies.append(pltpu.make_async_copy(link.at[:, s], tbuf.at[:, s], sems.at[2 * slabs + s]))
    for copy in copies:
        copy.start()
    eye = lax.broadcasted_iota(jnp.int32, (b, b), 0) == lax.broadcasted_iota(jnp.int32, (b, b), 1)
    e_dev = sigma.shape[0]
    at = (lax.axis_index("energy") * e_dev + energy).astype(F32)
    z = -1.0 + jnp.full((1, 1), 2.0 * at, F32) / (e_dev * n_energy)
    forward, adjoint_side, outward = [], [], []
    for s in range(slabs):
        copies[3 * s].wait()
        copies[3 * s + 1].wait()
        ar = jnp.where(eye, z, 0.0) - 0.5 * (hbuf[0, s] + hbuf[0, s].T) - sbuf[0, s]
        ai = jnp.where(eye, BROADENING, 0.0) - 0.5 * (hbuf[1, s] - hbuf[1, s].T) - sbuf[1, s]
        if s > 0:
            copies[3 * s - 1].wait()
            tr, ti = tbuf[0, s - 1], tbuf[1, s - 1]
            t_halves = halves((tr, ti))
            g_halves = halves(forward[-1])
            leaving = halves(complex_product(halves((tr.T, -ti.T)), g_halves))
            folded = complex_product(leaving, t_halves)
            ar, ai = ar - folded[0], ai - folded[1]
            adjoint_side.append(leaving)
            outward.append(halves(complex_product(g_halves, t_halves)))
        forward.append(newton_inverse(ar, ai, eye))
    block = forward[-1]
    place(early, late, (slabs - 1) * b, block)
    for s in range(slabs - 2, -1, -1):
        through = halves(complex_product(outward[s], halves(block)))
        closing = complex_product(through, adjoint_side[s])
        block = (forward[s][0] + closing[0], forward[s][1] + closing[1])
        place(early, late, s * b, block)


HBM = pl.BlockSpec(memory_space=pltpu.HBM)
VMEM = pl.BlockSpec(memory_space=pltpu.VMEM)
SMEM = pl.BlockSpec(memory_space=pltpu.SMEM)
CHEAP = pl.CostEstimate(flops=0, bytes_accessed=0, transcendentals=0)


def greens(energy, n_energy, earlier, ham, link, sigma, late_rows):
    _, slabs, b, _ = ham.shape
    return pl.pallas_call(
        after(earlier, functools.partial(greens_kernel, energy, n_energy)),
        out_shape=[
            jax.ShapeDtypeStruct((2 * b // LANES, slabs * b - late_rows, LANES), F32),
            jax.ShapeDtypeStruct((2 * b // LANES, late_rows, LANES), F32),
        ],
        in_specs=[ANY] * len(earlier) + [HBM, HBM, HBM],
        out_specs=[VMEM, VMEM],
        scratch_shapes=[
            pltpu.VMEM((2, slabs, b, b), F32),
            pltpu.VMEM((2, slabs - 1, b, b), F32),
            pltpu.VMEM((2, slabs, b, b), F32),
            pltpu.SemaphoreType.DMA((3 * slabs - 1,)),
        ],
        compiler_params=pltpu.CompilerParams(vmem_limit_bytes=GREENS_VMEM),
        cost_estimate=pl.CostEstimate(flops=10**11, bytes_accessed=4 * 10**6, transcendentals=0),
    )(*earlier, ham, link, sigma)


def row_loop(rows, step):
    def one(i, carry):
        step(pl.multiple_of(i * ROWS, ROWS))
        return carry

    lax.fori_loop(0, rows // ROWS, one, 0, unroll=UNROLL)


ANY = pl.BlockSpec(memory_space=pl.ANY)


def after(earlier, kernel):
    return lambda *refs: kernel(*refs[len(earlier) :])


def pointwise(earlier, kernel, shapes, specs, *args):
    return list(
        pl.pallas_call(
            after(earlier, kernel),
            out_shape=[jax.ShapeDtypeStruct(s, F32) for s in shapes],
            in_specs=[ANY] * len(earlier) + specs,
            out_specs=[VMEM] * len(shapes),
            compiler_params=pltpu.CompilerParams(vmem_limit_bytes=POINT_VMEM),
            cost_estimate=CHEAP,
        )(*earlier, *args)
    )


def weighted(out, terms):
    lead = out.shape[:-2]

    def step(at):
        rows = pl.ds(at, ROWS)
        for index in np.ndindex(*lead):
            total = None
            for scale, ref in terms:
                value = ref[(*index, rows)]
                value = value if scale is None else scale * value
                total = value if total is None else total + value
            out[(*index, rows)] = total

    row_loop(out.shape[-2], step)


def gathered_kernel(k_all, w, *refs):
    groups = k_all // 2
    held, mine, other = refs[:groups], refs[groups], refs[groups + 1 :]
    k = lax.axis_index("mom")
    each = mine.shape[0] // len(other)
    for i, out in enumerate((mine, *other)):
        to = k if i == 0 else k ^ 1
        terms = []
        for j, ref in enumerate(held):
            q = lax.rem(k - 2 * j + k_all, k_all)
            terms.append((w[to, q] / k_all, ref if i == 0 else ref.at[pl.ds((i - 1) * each, each)]))
        weighted(out, terms)


def paired_kernel(k_all, planes, w, *refs):
    xs, mates, outs = refs[:planes], refs[planes : 2 * planes], refs[2 * planes :]
    k = lax.axis_index("mom")
    e_dev = xs[0].shape[0]
    for i, out in enumerate(outs):
        to = lax.rem(k + 2 * (i // e_dev), k_all)
        for plane in range(planes):
            x, mate = xs[plane].at[i % e_dev], mates[plane].at[i % e_dev]
            weighted(out.at[plane], [(w[to, k] / k_all, x), (w[to, k ^ 1] / k_all, mate)])


def sum_kernel(x, *refs):
    outs = refs[-PIECES:]
    arrived = refs[:-PIECES]
    each, rows = arrived[0].shape[0], outs[0].shape[1]
    for piece, out in enumerate(outs):
        here = pl.ds(piece * rows, rows)
        for i, y in enumerate(arrived):
            planes = pl.ds(i * each, each)
            weighted(out.at[planes], [(None, x.at[planes, here]), (None, y.at[:, here])])


def phonon_rows(first_row, n_energy, b, shifts, bose, orbital, own, swapped, passed, write):
    modes, planes = orbital.shape[0], own[0].shape[0]
    e = lax.axis_index("energy")
    odd = lax.rem(e, 2) == 1
    edge = jnp.logical_or(e == 0, e == n_energy - 1)
    zero = jnp.float32(0.0)

    def scales(shift, down, up):
        out = []
        for m in range(modes):
            hit = shifts[m] == shift
            below = jnp.where(jnp.logical_and(hit, down), bose[m] + 1.0, zero)
            above = jnp.where(jnp.logical_and(hit, up), bose[m], zero)
            out.append(below + above)
        return out

    even = jnp.logical_not(odd)
    inner = jnp.logical_not(edge)
    lower, upper = jnp.logical_and(even, inner), jnp.logical_and(odd, inner)
    always, never = e >= 0, e < 0
    tables = [
        scales(1, always, never),
        scales(1, never, always),
        scales(2, odd, even),
        scales(1, odd, never),
        scales(1, never, even),
        scales(2, lower, upper),
        scales(1, lower, never),
        scales(1, never, upper),
    ]
    full = b // LANES

    def step(at):
        rows = pl.ds(at, ROWS)
        orbit = pl.ds(pl.multiple_of(lax.rem(at + first_row, b), ROWS), ROWS)
        for column in range(orbital.shape[1]):
            modes_here = [orbital[m, column, orbit] for m in range(modes)]
            down1, up1, s2, s1_low, s1_high, p2, p1_low, p1_high = [
                sum(s * v for s, v in zip(table, modes_here)) for table in tables
            ]
            for plane in [column, full + column] if column < full else [planes - 1]:
                oa, ob = own[0][plane, rows], own[1][plane, rows]
                sa, sb = swapped[0][plane, rows], swapped[1][plane, rows]
                pa, pb = passed[0][plane, rows], passed[1][plane, rows]
                write(0, plane, at, up1 * ob + s2 * sa + s1_low * sb + p2 * pa + p1_low * pb)
                write(1, plane, at, down1 * oa + s2 * sb + s1_high * sa + p2 * pb + p1_high * pa)

    row_loop(own[0].shape[1], step)


def late_phonon_kernel(first_row, n_energy, b, shifts, bose, orbital, oa, ob, sa, sb, pa, pb, *outs):
    def write(energy, plane, at, value):
        outs[plane][energy, pl.ds(at, ROWS)] = value

    phonon_rows(first_row, n_energy, b, shifts, bose, orbital, [oa, ob], [sa, sb], [pa, pb], write)


def store_unpacked(held, energy, at, planes):
    width = held.shape[-1]
    for part, pieces in enumerate(unpack(planes, width)):
        for lane, value in pieces:
            held[energy, part, pl.ds(at, ROWS), lane : lane + value.shape[-1]] = value


def late_out_kernel(first_row, count, *refs):
    arrived = refs[:count]
    out, held, sem = refs[-3:]
    energies, (planes, rows, _) = held.shape[0], arrived[0].shape

    def step(at):
        here = pl.ds(at, ROWS)
        for energy in range(energies):
            values = []
            for plane in range(planes):
                values.append(sum(ref[plane, here] for ref in arrived[energy::energies]))
            store_unpacked(held, energy, at, values)

    row_loop(rows, step)
    copy = pltpu.make_async_copy(held, out.at[:, :, pl.ds(first_row, rows)], sem)
    copy.start()
    copy.wait()


def early_out_kernel(n_energy, first_row, shifts, bose, orbital, oa, sa, pa, ob, sb, pb, *refs):
    out, held, sem = refs[-3:]
    rows, b = held.shape[2:]
    planes = oa.shape[0]
    got = {}

    def write(energy, plane, at, value):
        got[energy, plane] = value
        if plane == planes - 1:
            store_unpacked(held, energy, at, [got[energy, p] for p in range(planes)])

    phonon_rows(first_row, n_energy, b, shifts, bose, orbital, [oa, ob], [sa, sb], [pa, pb], write)
    copy = pltpu.make_async_copy(held, out.at[:, :, pl.ds(first_row, rows)], sem)
    copy.start()
    copy.wait()


def swap_pairs(x, axis):
    return lax.ppermute(x, axis, [(i, i ^ 1) for i in range(lax.axis_size(axis))])


def shift_groups(x, axis, step):
    n = lax.axis_size(axis)
    return lax.ppermute(x, axis, [(i, (i + 2 * step) % n) for i in range(n)])


def pass_on(x, axis):
    n = lax.axis_size(axis)
    return lax.ppermute(x, axis, [(i, (i + (2 if i % 2 == 0 else n - 2)) % n) for i in range(n)])


def body(hamiltonian, coupling, sigma_old, orbital_coupling, momentum_weights, bose_factor, shifts):
    k_all, n_energy = lax.axis_size("mom"), lax.axis_size("energy")
    e_dev, _, _, slabs, b, _ = sigma_old.shape
    groups = k_all // 2
    late_rows = b + b // 4
    early_rows = slabs * b - late_rows

    early, late = [], []
    earlier = []
    for e in range(e_dev):
        r, l = greens(e, n_energy, earlier, hamiltonian[0], coupling[0], sigma_old[:, 0], late_rows)
        early.append(r)
        late.append(l)
        earlier = [l]

    full = b - b % LANES
    columns = [orbital_coupling[..., at : at + LANES] for at in range(0, full, LANES)]
    if full < b:
        columns.append(jnp.concatenate([orbital_coupling[..., full:]] * 2, axis=-1))
    orbital = jnp.stack(columns, axis=1)

    planes, rows, lanes = early[0].shape

    def then(x, *earlier):
        return lax.optimization_barrier((x, *earlier))[0]

    def collect(x):
        return [x] + [shift_groups(x, "mom", j) for j in range(1, groups)]

    def gather(earlier, held):
        x = held[0]
        mine, *other = pointwise(
            earlier, functools.partial(gathered_kernel, k_all),
            [x.shape] + [(1, *x.shape[1:])] * planes,
            [SMEM] + [VMEM] * groups, momentum_weights, *held,
        )
        return mine, other

    def add_mate(earlier, mine, other):
        from_mate = [swap_pairs(x, "mom") for x in other]
        shapes = [(planes, rows // PIECES, lanes)] * PIECES
        return pointwise(earlier, sum_kernel, shapes, [VMEM] * (1 + len(other)), mine, *from_mate)

    late_swapped = [swap_pairs(late[0], "energy")]
    late_swapped.append(swap_pairs(then(late[1], late_swapped[0]), "energy"))
    late_passed = [pass_on(x, "energy") for x in late_swapped]
    held_a = collect(early[0])
    held_b = collect(then(early[1], *held_a[1:]))

    mine_a, other_a = gather([early[1]], held_a)
    mixed_a = add_mate([mine_a], mine_a, other_a)
    swapped_a = [swap_pairs(then(x, late_swapped[1]), "energy") for x in mixed_a]
    passed_a = [pass_on(swapped_a[0], "energy")]
    for x in swapped_a[1:]:
        passed_a.append(pass_on(then(x, passed_a[-1]), "energy"))
    mine_b, other_b = gather([mixed_a[0], swapped_a[0], late_passed[0]], held_b)
    mixed_b = add_mate([mine_b, swapped_a[1]], mine_b, other_b)
    swapped_b = [swap_pairs(x, "energy") for x in mixed_b]
    passed_b = [pass_on(then(swapped_b[0], passed_a[-1]), "energy")]
    for x in swapped_b[1:]:
        passed_b.append(pass_on(x, "energy"))
    late_sum = pointwise(
        [mixed_b[0]], functools.partial(late_phonon_kernel, early_rows, n_energy, b),
        [(e_dev, late_rows, lanes)] * planes, [SMEM, SMEM] + [VMEM] * 7,
        shifts, bose_factor, orbital, *late, *late_swapped, *late_passed,
    )
    mate = [swap_pairs(x, "mom") for x in late_sum]
    sends = pointwise(
        [], functools.partial(paired_kernel, k_all, planes),
        [late[0].shape] * (groups * e_dev), [SMEM] + [VMEM] * (2 * planes), momentum_weights, *late_sum, *mate,
    )
    arrived = [x if i < e_dev else shift_groups(x, "mom", i // e_dev) for i, x in enumerate(sends)]

    whole = (e_dev, 2, slabs * b, b)
    def write_out(kernel, rows, operands, specs, out=None):
        given = [] if out is None else [out]
        return pl.pallas_call(
            kernel,
            out_shape=jax.ShapeDtypeStruct(whole, F32),
            in_specs=specs + [HBM] * len(given),
            out_specs=HBM,
            scratch_shapes=[pltpu.VMEM((e_dev, 2, rows, b), F32), pltpu.SemaphoreType.DMA],
            input_output_aliases={len(operands): 0} if given else {},
            compiler_params=pltpu.CompilerParams(vmem_limit_bytes=POINT_VMEM),
            cost_estimate=CHEAP,
        )(*operands, *given)

    def early_out(i, out):
        operands = [shifts, bose_factor, orbital]
        operands += [x[i] for x in (mixed_a, swapped_a, passed_a, mixed_b, swapped_b, passed_b)]
        kernel = functools.partial(early_out_kernel, n_energy, i * (rows // PIECES))
        return write_out(kernel, rows // PIECES, operands, [SMEM, SMEM] + [VMEM] * 7, out)

    out = None
    for i in range(PIECES - 1):
        out = early_out(i, out)
    late_kernel = functools.partial(late_out_kernel, early_rows, len(arrived))
    out = write_out(late_kernel, late_rows, arrived, [VMEM] * len(arrived), out)
    out = early_out(PIECES - 1, out)
    return out.reshape(e_dev, 1, 2, slabs, b, b)


def solution(mesh):
    return jax.shard_map(
        body,
        mesh=mesh,
        in_specs=(
            P("mom", None, None, None, None),
            P("mom", None, None, None, None),
            P("energy", "mom", None, None, None, None),
            P(),
            P(),
            P(),
            P(),
        ),
        out_specs=P("energy", "mom", None, None, None, None),
        check_vma=False,
    )
```
